32 devices in a mesh: groups: 2 (over y), dp: 4 (over x, core), owner: 4 (over z).
Axes of the slice: x: 2, y: 2, z: 4, core: 2. Of those that a mesh axis runs over, the one named last changes fastest.
Arguments:
- hidden_act: bfloat16 [4096, 28672], P(('groups', 'dp'), 'owner'), parts along dimension 0, may hold values from -6 to 6
- out_grad: bfloat16 [4096, 8192], P(('groups', 'dp'), 'owner'), parts along dimension 0, may hold values from -6 to 6
- query_left: bfloat16 [32, 8, 8192], P('dp', None, 'owner'), may hold values from -0.0078125 to 0.0078125
- query_right: bfloat16 [32, 8, 28672], P('dp', None, 'owner'), may hold values from -0.00390625 to 0.00390625
- panel_live: int32 [8, 4], P(('groups', 'dp')), parts along dimension 0, may hold values from 1 to 128, as said below
- panel_example: int32 [8, 4], P(('groups', 'dp')), parts along dimension 0, may hold values from 0 to 1, never falling along the last dimension, each value on 1 to 3 neighbouring positions
Outputs:
- scores: float32 [16, 32], P(('groups', 'dp')), parts along dimension 0
The draws below stay inside these ranges and needn't reach their ends.
There are 2 independent parts, one for each index of `groups`. The reference program is written for one: setup_inputs(seed, part) draws one part's arguments, and reference() takes and returns one part's arrays. A program takes and returns all parts, laid end to end along the dimension named above; an argument that names none is the same for every part. Nothing has to cross between parts.
Inputs may be any that keep to these rules, and one draw needn't show every extreme that they name: `panel_live`: the first panel of every batch is full; every other panel holds its live tokens at its start. `panel_example`: never falls along a batch's panels; every id of 0 to 1 appears in every batch.
All inputs are finite; a program needn't handle non-finite values.
Results may differ from the reference program's by a relative error of at most 0.0003.
Values may be sent and summed in bfloat16 or wider, within the bound.
A program may use at most 64 MiB of HBM per device.

```python
import math
import jax
import jax.numpy as jnp
import numpy as np
from jax import lax

D = 8192
FF = 28672
PANEL = 128
PAN_DEV = 4
RANK = 8
TOK_DEV = 512
EX_DEV = 2
BATCHES = 4
TOKENS = 2048
EXAMPLES = 8
QRY = 32


def draw_panel_live(key, part):
    key = jax.random.fold_in(key, 11)
    counts = jax.random.randint(key, (BATCHES, PAN_DEV), 1, PANEL + 1)
    column = jnp.arange(PAN_DEV, dtype=jnp.int32)[None, :]
    return jnp.where(column == 0, PANEL, counts).astype(jnp.int32)


def level_of(key, dims, shards, smallest, largest):
    loudness = 1.0
    for dim, blocks in shards:
        steps = jax.random.uniform(jax.random.fold_in(jax.random.fold_in(key, 6), dim), (blocks,), jnp.float32, smallest / len(shards), largest / len(shards))
        loudness = loudness * jnp.repeat(jnp.exp(steps), dims[dim] // blocks).reshape((-1,) + (1,) * (len(dims) - 1 - dim))
    return loudness


def profile(number_of, total, bound, skew):
    loads = [(1 << 20) // math.isqrt(grade ** skew) + 1 for grade in range(2, number_of + 1)]
    surplus, holding = total - bound - (number_of - 1), [1] * (number_of - 1)
    while surplus > 0:
        movable = [i for i in range(number_of - 1) if holding[i] < bound]
        whole, remaining = sum([loads[i] for i in movable]), surplus
        for i in movable:
            more = min(bound - holding[i], max(1, remaining * loads[i] // whole), surplus)
            holding[i] = holding[i] + more
            surplus = surplus - more
    return np.array([bound] + holding)


def uneven(key, amount, total, most, skew):
    if amount == 2:
        one = jax.random.randint(key, (), max(1, total - most), min(most, total - 1) + 1)
        return jnp.stack([one, total - one])
    sizes = jnp.asarray(profile(amount, total, most, skew), jnp.int32)
    couples = (amount - 1) // 2
    source_of, taker = sizes[1:1 + 2 * couples:2], sizes[2:2 + 2 * couples:2]
    margin = jnp.minimum(source_of - 1, most - taker)
    shifted = jax.random.randint(jax.random.fold_in(key, 1), (couples,), 0, 1 << 20) % (margin + 1)
    sizes = sizes.at[1:1 + 2 * couples:2].set(source_of - shifted).at[2:2 + 2 * couples:2].set(taker + shifted)
    return sizes[jax.random.permutation(jax.random.fold_in(key, 2), amount)]


def gaussian(rng, extent, deviation, bound, split=(), held_as=jnp.bfloat16):
    result = deviation * jax.random.normal(rng, extent, jnp.float32)
    if split:
        result = result * level_of(rng, extent, split, -0.22, 0.18)
    return jnp.clip(result, -bound, bound).astype(held_as)


def setup_inputs(seed: int = 0, part: int = 0) -> dict:
    key_of = jax.random.split(jax.random.key(seed), 7)
    part_splits = jax.random.split(jax.random.fold_in(key_of[6], part), 7)
    return {
        "hidden_act": gaussian(part_splits[0], (TOKENS, FF), 1.0, 6.0, ((0, 4), (1, 4))),
        "out_grad": gaussian(part_splits[1], (TOKENS, D), 1.0, 6.0, ((0, 4), (1, 4))),
        "query_left": gaussian(key_of[2], (QRY, RANK, D), (64 * D) ** -0.5, 0.0078125, ((0, 4), (2, 4))),
        "query_right": gaussian(key_of[3], (QRY, RANK, FF), (64 * FF) ** -0.5, 0.00390625, ((0, 4), (2, 4))),
        "panel_live": draw_panel_live(jax.random.fold_in(jax.random.fold_in(key_of[6], part), 71), part),
        "panel_example": jax.vmap(lambda own: jnp.searchsorted(jnp.cumsum(uneven(own, EX_DEV, PAN_DEV, PAN_DEV - EX_DEV + 1, 1)), jnp.arange(PAN_DEV), side="right"))(jax.random.split(part_splits[5], BATCHES)).reshape((BATCHES, PAN_DEV)).astype(jnp.int32),
    }


def token_weights(panel_live, panel_example):
    position = jnp.arange(PANEL, dtype=jnp.int32)
    alive = (position[None, None, :] < panel_live[:, :, None]).astype(jnp.float32)
    labels = jnp.arange(EX_DEV, dtype=jnp.int32)
    onehot = (panel_example[:, :, None] == labels[None, None, :]).astype(jnp.float32)
    weight = alive[:, :, :, None] * onehot[:, :, None, :]
    return weight.reshape(BATCHES, TOK_DEV, EX_DEV)


def reference(hidden_act, out_grad, query_left, query_right, panel_live, panel_example):
    left = query_left.reshape(QRY * RANK, D)
    right = query_right.reshape(QRY * RANK, FF)
    left_proj = jnp.dot(out_grad, left.T, preferred_element_type=jnp.float32)
    right_proj = jnp.dot(hidden_act, right.T, preferred_element_type=jnp.float32)
    token_score = jnp.sum((left_proj * right_proj).reshape(TOKENS, QRY, RANK), axis=2)
    weight = token_weights(panel_live, panel_example)
    per_batch = token_score.reshape(BATCHES, TOK_DEV, QRY)
    scores = jnp.einsum("bte,btq->beq", weight, per_batch, precision=lax.Precision.HIGHEST)
    return scores.reshape(EXAMPLES, QRY)
```

```python
import functools

import jax
import jax.numpy as jnp
from jax import lax
from jax.experimental import pallas as pl
from jax.experimental.pallas import tpu as pltpu
from jax.sharding import PartitionSpec as P

PANEL = 128
EX_DEV = 2
SUB = 16
F32 = jnp.float32


def remote(src, dst, send_sem, recv_sem, device):
    return pltpu.make_async_remote_copy(
        src_ref=src,
        dst_ref=dst,
        send_sem=send_sem,
        recv_sem=recv_sem,
        device_id=device,
        device_id_type=pl.DeviceIdType.MESH,
    )


def matmul_nt(a, b):
    return lax.dot_general(a, b, (((1,), (1,)), ((), ())), preferred_element_type=F32)


def kernel(
    dims,
    act_hbm,
    grad_hbm,
    ql_hbm,
    qr_hbm,
    live_ref,
    example_ref,
    out_ref,
    act,
    grad,
    ql,
    qr,
    first,
    first_in,
    unit,
    unit_in,
    sums,
    ends,
    load_sem,
    own_sem,
    sib_send,
    sib_recv,
    x_send,
    x_recv,
    xs_send,
    xs_recv,
    y_send,
    y_recv,
    ys_send,
    ys_recv,
    z_send,
    z_recv,
    end_send,
    end_recv,
):
    chips, owners, splits = dims
    pieces = splits + 1
    tokens = act.shape[0]
    panels = tokens // PANEL
    half = panels // 2
    width = act.shape[1] // splits
    g = lax.axis_index("groups")
    d = lax.axis_index("dp")
    o = lax.axis_index("owner")
    x = d // 2
    core = d % 2
    sibling = {"dp": 2 * x + 1 - core}
    across = {"groups": 1 - g}

    def columns(f):
        return pl.ds((f - 1) * width, width)

    def block(s, h, a, f):
        return ql.at[s, h, a] if f == 0 else qr.at[s, h, a, :, columns(f)]

    def whole_block(s, f):
        return ql.at[s] if f == 0 else qr.at[s, :, :, :, columns(f)]

    own_loads = [
        pltpu.make_async_copy(ql_hbm, ql.at[d], own_sem.at[0]),
        pltpu.make_async_copy(qr_hbm, qr.at[d], own_sem.at[1]),
    ]
    for copy in own_loads:
        copy.start()
    loads = [pltpu.make_async_copy(grad_hbm, grad, load_sem.at[0])]
    for f in range(1, pieces):
        loads.append(
            pltpu.make_async_copy(act_hbm.at[:, columns(f)], act.at[:, columns(f)], load_sem.at[f])
        )
    for copy in loads:
        copy.start()

    barrier = pltpu.get_barrier_semaphore()
    peers = [sibling, across]
    peers += [{"dp": 2 * lax.rem(x + k, chips) + core} for k in range(1, chips)]
    peers += [{"owner": lax.rem(o + k, owners)} for k in range(1, owners)]
    for peer in peers:
        pl.semaphore_signal(barrier, inc=1, device_id=peer, device_id_type=pl.DeviceIdType.MESH)
    sums[...] = jnp.zeros_like(sums)
    for copy in own_loads:
        copy.wait()
    pl.semaphore_wait(barrier, len(peers))

    sends = []

    def send(src, dst, send_sem, recv_sem, device):
        copy = remote(src, dst, send_sem, recv_sem, device)
        copy.start()
        sends.append(copy)

    def arrived(ref, send_sem, recv_sem, device):
        remote(ref, ref, send_sem, recv_sem, device).wait_recv()

    order = [(k, a, f) for k in range(1, chips) for a in range(2) for f in range(pieces)]
    count = len(order)
    for f in range(pieces):
        if f < count:
            k, a, p = order[f]
            ref = block(d, g, a, p)
            send(ref, ref, x_send.at[f], x_recv.at[f], {"dp": 2 * lax.rem(x + k, chips) + core})
        ref = whole_block(d, f)
        send(ref, ref, sib_send.at[f], sib_recv.at[f], sibling)
    for i in range(pieces, count):
        k, a, p = order[i]
        ref = block(d, g, a, p)
        send(ref, ref, x_send.at[i], x_recv.at[i], {"dp": 2 * lax.rem(x + k, chips) + core})

    def chip_of(k):
        return lax.rem(x + chips - k, chips)

    def partial(u):
        return (first, first_in) if u == 0 else (unit.at[u - 1], unit_in.at[u - 1])

    def line_step(u, j, up):
        total, incoming = partial(u)
        lanes = total.shape[1]
        target = {"owner": lax.rem(o + 1, owners) if up else lax.rem(o + owners - 1, owners)}
        for sub in range(half):
            p = half + sub if up else sub
            rows = pl.ds(p * PANEL, PANEL)
            slot = u * panels + p
            if j > 0:
                arrived(incoming.at[rows], z_send.at[slot], z_recv.at[slot], target)
            if 0 < j < owners - 1:
                total[rows, :] = total[rows, :] + incoming[rows, :]
            if j < owners - 1:
                remote(
                    total.at[rows], incoming.at[rows], z_send.at[slot], z_recv.at[slot], target
                ).start()
            else:
                value = total[rows, :] + incoming[rows, :]
                if lanes == 256:
                    product = value[:, :128] * value[:, 128:]
                else:
                    product = value * pltpu.roll(value, 64, 1)
                position = lax.broadcasted_iota(jnp.int32, (PANEL, 128), 0)
                kept = jnp.where(position < live_ref[0, p], product, 0.0)
                row = jnp.sum(kept, axis=0, keepdims=True)
                label = lax.broadcasted_iota(jnp.int32, (8, 128), 0)
                sums[u] = sums[u] + jnp.where(label == example_ref[0, p], row, 0.0)

    def line(u, j):
        @pl.when(o == owners - 1 - j)
        def _():
            line_step(u, j, False)

        @pl.when(o == j)
        def _():
            line_step(u, j, True)

    units = 1 + 2 * (chips - 1)
    events = {}
    for u in range(units):
        ready = pieces - 1 if u == 0 else pieces * u + 1
        last = u == units - 1
        for j in range(owners):
            at = ready + (j if last else 2 * j)
            events.setdefault(at, []).append((u, j))

    for i in range(max(events) + 1):
        if i < count:
            k, a, f = order[i]
            ref = block(2 * chip_of(k) + core, g, a, f)
            arrived(ref, x_send.at[i], x_recv.at[i], sibling)
            send(ref, ref, y_send.at[i], y_recv.at[i], across)
            send(ref, ref, xs_send.at[i], xs_recv.at[i], sibling)
        if 1 <= i <= count:
            k, a, f = order[i - 1]
            ref = block(2 * chip_of(k) + core, 1 - g, a, f)
            arrived(ref, y_send.at[i - 1], y_recv.at[i - 1], across)
            send(ref, ref, ys_send.at[i - 1], ys_recv.at[i - 1], sibling)
        if i < pieces:
            loads[i].wait()
            arrived(
                whole_block(2 * x + 1 - core, i), sib_send.at[i], sib_recv.at[i], sibling
            )
            if i == 0:
                rhs = ql[pl.ds(2 * x, 2)].reshape(128, ql.shape[-1])
                first[:, :128] = matmul_nt(grad[...], rhs)
            else:
                cols = columns(i)
                rhs = qr[pl.ds(2 * x, 2), :, :, :, cols].reshape(128, width)
                part = matmul_nt(act[:, cols], rhs)
                first[:, 128:] = part if i == 1 else first[:, 128:] + part
        if 2 <= i < count + 2:
            k, a, f = order[i - 2]
            source = chip_of(k)
            other = 2 * source + 1 - core
            arrived(block(other, g, a, f), xs_send.at[i - 2], xs_recv.at[i - 2], sibling)
            arrived(block(other, 1 - g, a, f), ys_send.at[i - 2], ys_recv.at[i - 2], sibling)
            u = 2 * (k - 1) + a
            if f == 0:
                rhs = ql[pl.ds(2 * source, 2), :, a].reshape(64, ql.shape[-1])
                rhs = jnp.concatenate([rhs, jnp.zeros_like(rhs)], axis=0)
                unit[u] = matmul_nt(grad[...], rhs)
            else:
                cols = columns(f)
                rhs = qr[pl.ds(2 * source, 2), :, a, :, cols].reshape(64, width)
                rhs = jnp.concatenate([jnp.zeros_like(rhs), rhs], axis=0)
                unit[u] = unit[u] + matmul_nt(act[:, cols], rhs)
        for u, j in events.get(i, ()):
            line(u, j)

    def end_copies(e):
        return [
            remote(
                ends.at[e],
                ends.at[e],
                end_send.at[e, k],
                end_recv.at[e],
                {"owner": lax.rem(o + k, owners)},
            )
            for k in range(1, owners)
        ]

    lane = lax.broadcasted_iota(jnp.int32, (128, ends.shape[-1]), 0)
    query = lax.broadcasted_iota(jnp.int32, (128, ends.shape[-1]), 1)
    for e in range(2):

        @pl.when(o == (owners - 1) * e)
        def _(e=e):
            spread = (query == 16 * x + lane // 8).astype(F32)
            result = jnp.dot(
                sums[0], spread, precision=lax.Precision.HIGHEST, preferred_element_type=F32
            )
            for k in range(1, chips):
                for a in range(2):
                    u = 1 + 2 * (k - 1) + a
                    place = (lane // 32) * 8 + (lane % 32) // 16 * 4 + 2 * a + (lane % 16) // 8
                    hit = (query == 16 * chip_of(k) + place) & (lane < 64)
                    result = result + jnp.dot(
                        sums[u],
                        hit.astype(F32),
                        precision=lax.Precision.HIGHEST,
                        preferred_element_type=F32,
                    )
            ends[e] = result
            for copy in end_copies(e):
                copy.start()

    for e in range(2):

        @pl.when(o != (owners - 1) * e)
        def _(e=e):
            arrived(ends.at[e], end_send.at[e, 1], end_recv.at[e], sibling)

    both = ends[0] + ends[1]
    out_ref[...] = both[: out_ref.shape[0], : out_ref.shape[1]]

    for copy in sends:
        copy.wait_send()
    for u in range(units):
        total, incoming = partial(u)
        for p in range(panels):
            rows = pl.ds(p * PANEL, PANEL)
            slot = u * panels + p

            @pl.when(o < owners - 1 if p >= half else o > 0)
            def _(total=total, incoming=incoming, rows=rows, slot=slot):
                remote(
                    total.at[rows], incoming.at[rows], z_send.at[slot], z_recv.at[slot], sibling
                ).wait_send()

    for e in range(2):

        @pl.when(o == (owners - 1) * e)
        def _(e=e):
            for copy in end_copies(e):
                copy.wait_send()


def shards(sizes, hidden_act, out_grad, query_left, query_right, panel_live, panel_example):
    chips, owners = sizes
    tokens, units_here = hidden_act.shape
    feat_here = out_grad.shape[1]
    block, ranks, _ = query_left.shape
    splits = 4 if chips == 2 else 1
    pieces = splits + 1
    count = 2 * (chips - 1) * pieces
    units = 1 + 2 * (chips - 1)
    queries = block * 2 * chips
    wide = -(-queries // 128) * 128
    panels = tokens // PANEL
    ql = query_left.reshape(2, 2, SUB, feat_here)
    qr = query_right.reshape(2, 2, SUB, units_here)
    dma = pltpu.SemaphoreType.DMA
    anywhere = pl.BlockSpec(memory_space=pl.ANY)
    smem = pl.BlockSpec(memory_space=pltpu.SMEM)
    return pl.pallas_call(
        functools.partial(kernel, (chips, owners, splits)),
        out_shape=jax.ShapeDtypeStruct((EX_DEV, queries), F32),
        in_specs=[anywhere] * 4 + [smem] * 2,
        out_specs=pl.BlockSpec(memory_space=pltpu.VMEM),
        scratch_shapes=[
            pltpu.VMEM((tokens, units_here), jnp.bfloat16),
            pltpu.VMEM((tokens, feat_here), jnp.bfloat16),
            pltpu.VMEM((2 * chips, 2, 2, SUB, feat_here), jnp.bfloat16),
            pltpu.VMEM((2 * chips, 2, 2, SUB, units_here), jnp.bfloat16),
            pltpu.VMEM((tokens, 256), F32),
            pltpu.VMEM((tokens, 256), F32),
            pltpu.VMEM((units - 1, tokens, 128), F32),
            pltpu.VMEM((units - 1, tokens, 128), F32),
            pltpu.VMEM((units, 8, 128), F32),
            pltpu.VMEM((2, 8, wide), F32),
            dma((pieces,)),
            dma((2,)),
            dma((pieces,)),
            dma((pieces,)),
        ]
        + [dma((count,))] * 8
        + [
            dma((units * panels,)),
            dma((units * panels,)),
            dma((2, owners)),
            dma((2,)),
        ],
        compiler_params=pltpu.CompilerParams(
            collective_id=0, has_side_effects=True, vmem_limit_bytes=56 * 1024 * 1024
        ),
    )(hidden_act, out_grad, ql, qr, panel_live, panel_example)


def solution(mesh):
    sizes = (mesh.shape["dp"] // 2, mesh.shape["owner"])
    return jax.shard_map(
        functools.partial(shards, sizes),
        mesh=mesh,
        in_specs=(
            P(("groups", "dp"), "owner"),
            P(("groups", "dp"), "owner"),
            P("dp", None, "owner"),
            P("dp", None, "owner"),
            P(("groups", "dp"), None),
            P(("groups", "dp"), None),
        ),
        out_specs=P(("groups", "dp"), None),
        check_vma=False,
    )
```

```python
import functools

import jax
import jax.numpy as jnp
from jax import lax
from jax.experimental import pallas as pl
from jax.experimental.pallas import tpu as pltpu
from jax.sharding import PartitionSpec as P

PANEL = 128
EX_DEV = 2
SUB = 16
LOOK = 2
EARLY = 2
F32 = jnp.float32


def remote(src, dst, send_sem, recv_sem, device):
    return pltpu.make_async_remote_copy(
        src_ref=src,
        dst_ref=dst,
        send_sem=send_sem,
        recv_sem=recv_sem,
        device_id=device,
        device_id_type=pl.DeviceIdType.MESH,
    )


def matmul_nt(a, b):
    return lax.dot_general(a, b, (((1,), (1,)), ((), ())), preferred_element_type=F32)


def kernel(
    dims,
    act_hbm,
    grad_hbm,
    ql_hbm,
    qr_hbm,
    live_ref,
    example_ref,
    out_ref,
    act,
    grad,
    ql,
    qr,
    first,
    first_in,
    unit,
    unit_in,
    sums,
    ends,
    load_sem,
    own_sem,
    sib_send,
    sib_recv,
    x_send,
    x_recv,
    xs_send,
    xs_recv,
    y_send,
    y_recv,
    ys_send,
    ys_recv,
    z_send,
    z_recv,
    end_send,
    end_recv,
):
    chips, owners, splits = dims
    pieces = splits + 1
    tokens = act.shape[0]
    share = tokens // owners
    width = act.shape[1] // splits
    g = lax.axis_index("groups")
    d = lax.axis_index("dp")
    o = lax.axis_index("owner")
    x = d // 2
    core = d % 2
    sibling = {"dp": 2 * x + 1 - core}
    across = {"groups": 1 - g}

    def columns(f):
        return pl.ds((f - 1) * width, width)

    def block(s, h, a, f):
        return ql.at[s, h, a] if f == 0 else qr.at[s, h, a, :, columns(f)]

    def whole_block(s, f):
        return ql.at[s] if f == 0 else qr.at[s, :, :, :, columns(f)]

    own_loads = [
        pltpu.make_async_copy(ql_hbm, ql.at[d], own_sem.at[0]),
        pltpu.make_async_copy(qr_hbm, qr.at[d], own_sem.at[1]),
    ]
    for copy in own_loads:
        copy.start()
    loads = [pltpu.make_async_copy(grad_hbm, grad, load_sem.at[0])]
    for f in range(1, pieces):
        loads.append(
            pltpu.make_async_copy(act_hbm.at[:, columns(f)], act.at[:, columns(f)], load_sem.at[f])
        )
    for copy in loads[:EARLY]:
        copy.start()

    barrier = pltpu.get_barrier_semaphore()
    peers = [sibling, across]
    peers += [{"dp": 2 * lax.rem(x + k, chips) + core} for k in range(1, chips)]
    peers += [{"owner": lax.rem(o + k, owners)} for k in range(1, owners)]
    for peer in peers:
        pl.semaphore_signal(barrier, inc=1, device_id=peer, device_id_type=pl.DeviceIdType.MESH)
    sums[...] = jnp.zeros_like(sums)
    for copy in own_loads:
        copy.wait()
    pl.semaphore_wait(barrier, len(peers))

    sends = []

    def send(src, dst, send_sem, recv_sem, device):
        copy = remote(src, dst, send_sem, recv_sem, device)
        copy.start()
        sends.append(copy)

    def arrived(ref, send_sem, recv_sem, device):
        remote(ref, ref, send_sem, recv_sem, device).wait_recv()

    order = [(k, a, f) for k in range(1, chips) for a in range(2) for f in range(pieces)]
    count = len(order)

    def send_across_x(i):
        if i < count:
            k, a, p = order[i]
            ref = block(d, g, a, p)
            send(ref, ref, x_send.at[i], x_recv.at[i], {"dp": 2 * lax.rem(x + k, chips) + core})

    for i in range(LOOK):
        send_across_x(i)
    for f in range(pieces):
        ref = whole_block(d, f)
        send(ref, ref, sib_send.at[f], sib_recv.at[f], sibling)
    for copy in loads[EARLY:]:
        copy.start()

    def chip_of(k):
        return lax.rem(x + chips - k, chips)

    def partial(u):
        return (first, first_in) if u == 0 else (unit.at[u - 1], unit_in.at[u - 1])

    def z_peer(k):
        return lax.rem(o + k, owners)

    def z_copy(u, k):
        total, incoming = partial(u)
        slot = u * owners + k
        rows = pl.ds(pl.multiple_of(z_peer(k) * share, share), share)
        return remote(
            total.at[rows],
            incoming.at[k - 1],
            z_send.at[slot],
            z_recv.at[slot],
            {"owner": z_peer(k)},
        )

    def scatter(u):
        for k in range(1, owners):
            z_copy(u, k).start()

    def finish(u):
        total, incoming = partial(u)
        for k in range(1, owners):
            z_copy(u, k).wait_recv()
        value = total[pl.ds(pl.multiple_of(o * share, share), share), :]
        for k in range(1, owners):
            value = value + incoming[k - 1]
        if value.shape[1] == 256:
            product = value[:, :128] * value[:, 128:]
        else:
            product = value * pltpu.roll(value, 64, 1)
        for start in range(0, share, min(share, PANEL)):
            rows = min(share, PANEL)
            token = o * share + start
            panel = token // PANEL
            position = lax.broadcasted_iota(jnp.int32, (rows, 128), 0) + token % PANEL
            kept = jnp.where(position < live_ref[0, panel], product[start : start + rows], 0.0)
            row = jnp.sum(kept, axis=0, keepdims=True)
            label = lax.broadcasted_iota(jnp.int32, (8, 128), 0)
            sums[u] = sums[u] + jnp.where(label == example_ref[0, panel], row, 0.0)

    units = 1 + 2 * (chips - 1)
    ready = {pieces - 1: 0}
    for u in range(1, units):
        ready[pieces * u + 1] = u

    for i in range(max(ready) + 1):
        if i < count:
            k, a, f = order[i]
            ref = block(2 * chip_of(k) + core, g, a, f)
            arrived(ref, x_send.at[i], x_recv.at[i], sibling)
            send_across_x(i + LOOK)
            send(ref, ref, y_send.at[i], y_recv.at[i], across)
            send(ref, ref, xs_send.at[i], xs_recv.at[i], sibling)
        if 1 <= i <= count:
            k, a, f = order[i - 1]
            ref = block(2 * chip_of(k) + core, 1 - g, a, f)
            arrived(ref, y_send.at[i - 1], y_recv.at[i - 1], across)
            send(ref, ref, ys_send.at[i - 1], ys_recv.at[i - 1], sibling)
        if i < pieces:
            loads[i].wait()
            arrived(
                whole_block(2 * x + 1 - core, i), sib_send.at[i], sib_recv.at[i], sibling
            )
            if i == 0:
                rhs = ql[pl.ds(2 * x, 2)].reshape(128, ql.shape[-1])
                first[:, :128] = matmul_nt(grad[...], rhs)
            else:
                cols = columns(i)
                rhs = qr[pl.ds(2 * x, 2), :, :, :, cols].reshape(128, width)
                part = matmul_nt(act[:, cols], rhs)
                first[:, 128:] = part if i == 1 else first[:, 128:] + part
        if 2 <= i < count + 2:
            k, a, f = order[i - 2]
            source = chip_of(k)
            other = 2 * source + 1 - core
            arrived(block(other, g, a, f), xs_send.at[i - 2], xs_recv.at[i - 2], sibling)
            arrived(block(other, 1 - g, a, f), ys_send.at[i - 2], ys_recv.at[i - 2], sibling)
            u = 2 * (k - 1) + a
            if f == 0:
                rhs = ql[pl.ds(2 * source, 2), :, a].reshape(64, ql.shape[-1])
                rhs = jnp.concatenate([rhs, jnp.zeros_like(rhs)], axis=0)
                unit[u] = matmul_nt(grad[...], rhs)
            else:
                cols = columns(f)
                rhs = qr[pl.ds(2 * source, 2), :, a, :, cols].reshape(64, width)
                rhs = jnp.concatenate([jnp.zeros_like(rhs), rhs], axis=0)
                unit[u] = unit[u] + matmul_nt(act[:, cols], rhs)
        if i in ready:
            scatter(ready[i])

    for u in range(units):
        finish(u)

    lane = lax.broadcasted_iota(jnp.int32, (128, ends.shape[-1]), 0)
    query = lax.broadcasted_iota(jnp.int32, (128, ends.shape[-1]), 1)
    spread = (query == 16 * x + lane // 8).astype(F32)
    result = jnp.dot(
        sums[0], spread, precision=lax.Precision.HIGHEST, preferred_element_type=F32
    )
    for k in range(1, chips):
        for a in range(2):
            u = 1 + 2 * (k - 1) + a
            place = (lane // 32) * 8 + (lane % 32) // 16 * 4 + 2 * a + (lane % 16) // 8
            hit = (query == 16 * chip_of(k) + place) & (lane < 64)
            result = result + jnp.dot(
                sums[u],
                hit.astype(F32),
                precision=lax.Precision.HIGHEST,
                preferred_element_type=F32,
            )
    ends[o] = result
    end_copies = [
        remote(
            ends.at[o], ends.at[o], end_send.at[k], end_recv.at[k], {"owner": z_peer(k)}
        )
        for k in range(1, owners)
    ]
    for copy in end_copies:
        copy.start()
    for k in range(1, owners):
        arrived(ends.at[z_peer(owners - k)], end_send.at[k], end_recv.at[k], sibling)
    both = ends[0]
    for e in range(1, owners):
        both = both + ends[e]
    out_ref[...] = both[: out_ref.shape[0], : out_ref.shape[1]]

    for copy in sends:
        copy.wait_send()
    for u in range(units):
        for k in range(1, owners):
            z_copy(u, k).wait_send()
    for copy in end_copies:
        copy.wait_send()


def shards(sizes, hidden_act, out_grad, query_left, query_right, panel_live, panel_example):
    chips, owners = sizes
    tokens, units_here = hidden_act.shape
    feat_here = out_grad.shape[1]
    block, ranks, _ = query_left.shape
    splits = 4 if chips == 2 else 1
    pieces = splits + 1
    count = 2 * (chips - 1) * pieces
    units = 1 + 2 * (chips - 1)
    queries = block * 2 * chips
    wide = -(-queries // 128) * 128
    share = tokens // owners
    ql = query_left.reshape(2, 2, SUB, feat_here)
    qr = query_right.reshape(2, 2, SUB, units_here)
    dma = pltpu.SemaphoreType.DMA
    anywhere = pl.BlockSpec(memory_space=pl.ANY)
    smem = pl.BlockSpec(memory_space=pltpu.SMEM)
    return pl.pallas_call(
        functools.partial(kernel, (chips, owners, splits)),
        out_shape=jax.ShapeDtypeStruct((EX_DEV, queries), F32),
        in_specs=[anywhere] * 4 + [smem] * 2,
        out_specs=pl.BlockSpec(memory_space=pltpu.VMEM),
        scratch_shapes=[
            pltpu.VMEM((tokens, units_here), jnp.bfloat16),
            pltpu.VMEM((tokens, feat_here), jnp.bfloat16),
            pltpu.VMEM((2 * chips, 2, 2, SUB, feat_here), jnp.bfloat16),
            pltpu.VMEM((2 * chips, 2, 2, SUB, units_here), jnp.bfloat16),
            pltpu.VMEM((tokens, 256), F32),
            pltpu.VMEM((owners - 1, share, 256), F32),
            pltpu.VMEM((units - 1, tokens, 128), F32),
            pltpu.VMEM((units - 1, owners - 1, share, 128), F32),
            pltpu.VMEM((units, 8, 128), F32),
            pltpu.VMEM((owners, 8, wide), F32),
            dma((pieces,)),
            dma((2,)),
            dma((pieces,)),
            dma((pieces,)),
        ]
        + [dma((count,))] * 8
        + [
            dma((units * owners,)),
            dma((units * owners,)),
            dma((owners,)),
            dma((owners,)),
        ],
        compiler_params=pltpu.CompilerParams(
            collective_id=0, has_side_effects=True, vmem_limit_bytes=56 * 1024 * 1024
        ),
    )(hidden_act, out_grad, ql, qr, panel_live, panel_example)


def solution(mesh):
    sizes = (mesh.shape["dp"] // 2, mesh.shape["owner"])
    return jax.shard_map(
        functools.partial(shards, sizes),
        mesh=mesh,
        in_specs=(
            P(("groups", "dp"), "owner"),
            P(("groups", "dp"), "owner"),
            P("dp", None, "owner"),
            P("dp", None, "owner"),
            P(("groups", "dp"), None),
            P(("groups", "dp"), None),
        ),
        out_specs=P(("groups", "dp"), None),
        check_vma=False,
    )
```

```python
import functools

import jax
import jax.numpy as jnp
from jax import lax
from jax.experimental import pallas as pl
from jax.experimental.pallas import tpu as pltpu
from jax.sharding import PartitionSpec as P

PANEL = 128
EX_DEV = 2
SUB = 16
LOOK = 4
Y_LAG = 3
USE_LAG = 5
EARLY = 2
F32 = jnp.float32


def remote(src, dst, send_sem, recv_sem, device):
    return pltpu.make_async_remote_copy(
        src_ref=src,
        dst_ref=dst,
        send_sem=send_sem,
        recv_sem=recv_sem,
        device_id=device,
        device_id_type=pl.DeviceIdType.MESH,
    )


def matmul_nt(a, b):
    return lax.dot_general(a, b, (((1,), (1,)), ((), ())), preferred_element_type=F32)


def kernel(
    dims,
    act_hbm,
    grad_hbm,
    ql_hbm,
    qr_hbm,
    live_ref,
    example_ref,
    out_ref,
    act,
    grad,
    ql,
    qr,
    first,
    first_in,
    unit,
    unit_in,
    sums,
    ends,
    load_sem,
    own_sem,
    sib_send,
    sib_recv,
    x_send,
    x_recv,
    xs_send,
    xs_recv,
    y_send,
    y_recv,
    ys_send,
    ys_recv,
    z_send,
    z_recv,
    end_send,
    end_recv,
):
    chips, owners, splits = dims
    pieces = splits + 1
    tokens = act.shape[0]
    share = tokens // owners
    width = act.shape[1] // splits
    g = lax.axis_index("groups")
    d = lax.axis_index("dp")
    o = lax.axis_index("owner")
    x = d // 2
    core = d % 2
    sibling = {"dp": 2 * x + 1 - core}
    across = {"groups": 1 - g}

    def columns(f):
        return pl.ds((f - 1) * width, width)

    def block(s, h, a, f):
        return ql.at[s, h, a] if f == 0 else qr.at[s, h, a, :, columns(f)]

    def whole_block(s, f):
        return ql.at[s] if f == 0 else qr.at[s, :, :, :, columns(f)]

    own_loads = [
        pltpu.make_async_copy(ql_hbm, ql.at[d], own_sem.at[0]),
        pltpu.make_async_copy(qr_hbm, qr.at[d], own_sem.at[1]),
    ]
    for copy in own_loads:
        copy.start()
    loads = [pltpu.make_async_copy(grad_hbm, grad, load_sem.at[0])]
    for f in range(1, pieces):
        loads.append(
            pltpu.make_async_copy(act_hbm.at[:, columns(f)], act.at[:, columns(f)], load_sem.at[f])
        )
    for copy in loads[:EARLY]:
        copy.start()

    barrier = pltpu.get_barrier_semaphore()
    peers = [sibling, across]
    peers += [{"dp": 2 * lax.rem(x + k, chips) + core} for k in range(1, chips)]
    peers += [{"owner": lax.rem(o + k, owners)} for k in range(1, owners)]
    for peer in peers:
        pl.semaphore_signal(barrier, inc=1, device_id=peer, device_id_type=pl.DeviceIdType.MESH)
    sums[...] = jnp.zeros_like(sums)
    for copy in own_loads:
        copy.wait()
    pl.semaphore_wait(barrier, len(peers))

    sends = []

    def send(src, dst, send_sem, recv_sem, device):
        copy = remote(src, dst, send_sem, recv_sem, device)
        copy.start()
        sends.append(copy)

    def arrived(ref, send_sem, recv_sem, device):
        remote(ref, ref, send_sem, recv_sem, device).wait_recv()

    order = [(k, a, f) for k in range(1, chips) for a in range(2) for f in range(pieces)]
    count = len(order)

    def send_across_x(i):
        if i < count:
            k, a, p = order[i]
            ref = block(d, g, a, p)
            send(ref, ref, x_send.at[i], x_recv.at[i], {"dp": 2 * lax.rem(x + k, chips) + core})

    for i in range(LOOK):
        send_across_x(i)
    for f in range(pieces):
        ref = whole_block(d, f)
        send(ref, ref, sib_send.at[f], sib_recv.at[f], sibling)
    for copy in loads[EARLY:]:
        copy.start()

    def chip_of(k):
        return lax.rem(x + chips - k, chips)

    def partial(u):
        return (first, first_in) if u == 0 else (unit.at[u - 1], unit_in.at[u - 1])

    def z_peer(k):
        return lax.rem(o + k, owners)

    def z_copy(u, k):
        total, incoming = partial(u)
        slot = u * owners + k
        rows = pl.ds(pl.multiple_of(z_peer(k) * share, share), share)
        return remote(
            total.at[rows],
            incoming.at[k - 1],
            z_send.at[slot],
            z_recv.at[slot],
            {"owner": z_peer(k)},
        )

    def scatter(u):
        for k in range(1, owners):
            z_copy(u, k).start()

    def finish(u):
        total, incoming = partial(u)
        for k in range(1, owners):
            z_copy(u, k).wait_recv()
        value = total[pl.ds(pl.multiple_of(o * share, share), share), :]
        for k in range(1, owners):
            value = value + incoming[k - 1]
        if value.shape[1] == 256:
            product = value[:, :128] * value[:, 128:]
        else:
            product = value * pltpu.roll(value, 64, 1)
        for start in range(0, share, min(share, PANEL)):
            rows = min(share, PANEL)
            token = o * share + start
            panel = token // PANEL
            position = lax.broadcasted_iota(jnp.int32, (rows, 128), 0) + token % PANEL
            kept = jnp.where(position < live_ref[0, panel], product[start : start + rows], 0.0)
            row = jnp.sum(kept, axis=0, keepdims=True)
            label = lax.broadcasted_iota(jnp.int32, (8, 128), 0)
            sums[u] = sums[u] + jnp.where(label == example_ref[0, panel], row, 0.0)

    units = 1 + 2 * (chips - 1)
    ready = {pieces - 1: 0}
    for u in range(1, units):
        ready[pieces * u - 1 + USE_LAG] = u

    for i in range(max(ready) + 1):
        if i < count:
            k, a, f = order[i]
            ref = block(2 * chip_of(k) + core, g, a, f)
            arrived(ref, x_send.at[i], x_recv.at[i], sibling)
            send_across_x(i + LOOK)
            send(ref, ref, y_send.at[i], y_recv.at[i], across)
            send(ref, ref, xs_send.at[i], xs_recv.at[i], sibling)
        if Y_LAG <= i < count + Y_LAG:
            k, a, f = order[i - Y_LAG]
            ref = block(2 * chip_of(k) + core, 1 - g, a, f)
            arrived(ref, y_send.at[i - Y_LAG], y_recv.at[i - Y_LAG], across)
            send(ref, ref, ys_send.at[i - Y_LAG], ys_recv.at[i - Y_LAG], sibling)
        if i < pieces:
            loads[i].wait()
            arrived(
                whole_block(2 * x + 1 - core, i), sib_send.at[i], sib_recv.at[i], sibling
            )
            if i == 0:
                rhs = ql[pl.ds(2 * x, 2)].reshape(128, ql.shape[-1])
                first[:, :128] = matmul_nt(grad[...], rhs)
            else:
                cols = columns(i)
                rhs = qr[pl.ds(2 * x, 2), :, :, :, cols].reshape(128, width)
                part = matmul_nt(act[:, cols], rhs)
                first[:, 128:] = part if i == 1 else first[:, 128:] + part
        if USE_LAG <= i < count + USE_LAG:
            k, a, f = order[i - USE_LAG]
            source = chip_of(k)
            other = 2 * source + 1 - core
            arrived(block(other, g, a, f), xs_send.at[i - USE_LAG], xs_recv.at[i - USE_LAG], sibling)
            arrived(block(other, 1 - g, a, f), ys_send.at[i - USE_LAG], ys_recv.at[i - USE_LAG], sibling)
            u = 2 * (k - 1) + a
            if f == 0:
                rhs = ql[pl.ds(2 * source, 2), :, a].reshape(64, ql.shape[-1])
                rhs = jnp.concatenate([rhs, jnp.zeros_like(rhs)], axis=0)
                unit[u] = matmul_nt(grad[...], rhs)
            else:
                cols = columns(f)
                rhs = qr[pl.ds(2 * source, 2), :, a, :, cols].reshape(64, width)
                rhs = jnp.concatenate([jnp.zeros_like(rhs), rhs], axis=0)
                unit[u] = unit[u] + matmul_nt(act[:, cols], rhs)
        if i in ready:
            scatter(ready[i])

    for u in range(units):
        finish(u)

    lane = lax.broadcasted_iota(jnp.int32, (128, ends.shape[-1]), 0)
    query = lax.broadcasted_iota(jnp.int32, (128, ends.shape[-1]), 1)
    spread = (query == 16 * x + lane // 8).astype(F32)
    result = jnp.dot(
        sums[0], spread, precision=lax.Precision.HIGHEST, preferred_element_type=F32
    )
    for k in range(1, chips):
        for a in range(2):
            u = 1 + 2 * (k - 1) + a
            place = (lane // 32) * 8 + (lane % 32) // 16 * 4 + 2 * a + (lane % 16) // 8
            hit = (query == 16 * chip_of(k) + place) & (lane < 64)
            result = result + jnp.dot(
                sums[u],
                hit.astype(F32),
                precision=lax.Precision.HIGHEST,
                preferred_element_type=F32,
            )
    ends[o] = result
    end_copies = [
        remote(
            ends.at[o], ends.at[o], end_send.at[k], end_recv.at[k], {"owner": z_peer(k)}
        )
        for k in range(1, owners)
    ]
    for copy in end_copies:
        copy.start()
    for k in range(1, owners):
        arrived(ends.at[z_peer(owners - k)], end_send.at[k], end_recv.at[k], sibling)
    both = ends[0]
    for e in range(1, owners):
        both = both + ends[e]
    out_ref[...] = both[: out_ref.shape[0], : out_ref.shape[1]]

    for copy in sends:
        copy.wait_send()
    for u in range(units):
        for k in range(1, owners):
            z_copy(u, k).wait_send()
    for copy in end_copies:
        copy.wait_send()


def shards(sizes, hidden_act, out_grad, query_left, query_right, panel_live, panel_example):
    chips, owners = sizes
    tokens, units_here = hidden_act.shape
    feat_here = out_grad.shape[1]
    block, ranks, _ = query_left.shape
    splits = 4 if chips == 2 else 1
    pieces = splits + 1
    count = 2 * (chips - 1) * pieces
    units = 1 + 2 * (chips - 1)
    queries = block * 2 * chips
    wide = -(-queries // 128) * 128
    share = tokens // owners
    ql = query_left.reshape(2, 2, SUB, feat_here)
    qr = query_right.reshape(2, 2, SUB, units_here)
    dma = pltpu.SemaphoreType.DMA
    anywhere = pl.BlockSpec(memory_space=pl.ANY)
    smem = pl.BlockSpec(memory_space=pltpu.SMEM)
    return pl.pallas_call(
        functools.partial(kernel, (chips, owners, splits)),
        out_shape=jax.ShapeDtypeStruct((EX_DEV, queries), F32),
        in_specs=[anywhere] * 4 + [smem] * 2,
        out_specs=pl.BlockSpec(memory_space=pltpu.VMEM),
        scratch_shapes=[
            pltpu.VMEM((tokens, units_here), jnp.bfloat16),
            pltpu.VMEM((tokens, feat_here), jnp.bfloat16),
            pltpu.VMEM((2 * chips, 2, 2, SUB, feat_here), jnp.bfloat16),
            pltpu.VMEM((2 * chips, 2, 2, SUB, units_here), jnp.bfloat16),
            pltpu.VMEM((tokens, 256), F32),
            pltpu.VMEM((owners - 1, share, 256), F32),
            pltpu.VMEM((units - 1, tokens, 128), F32),
            pltpu.VMEM((units - 1, owners - 1, share, 128), F32),
            pltpu.VMEM((units, 8, 128), F32),
            pltpu.VMEM((owners, 8, wide), F32),
            dma((pieces,)),
            dma((2,)),
            dma((pieces,)),
            dma((pieces,)),
        ]
        + [dma((count,))] * 8
        + [
            dma((units * owners,)),
            dma((units * owners,)),
            dma((owners,)),
            dma((owners,)),
        ],
        compiler_params=pltpu.CompilerParams(
            collective_id=0, has_side_effects=True, vmem_limit_bytes=56 * 1024 * 1024
        ),
    )(hidden_act, out_grad, ql, qr, panel_live, panel_example)


def solution(mesh):
    sizes = (mesh.shape["dp"] // 2, mesh.shape["owner"])
    return jax.shard_map(
        functools.partial(shards, sizes),
        mesh=mesh,
        in_specs=(
            P(("groups", "dp"), "owner"),
            P(("groups", "dp"), "owner"),
            P("dp", None, "owner"),
            P("dp", None, "owner"),
            P(("groups", "dp"), None),
            P(("groups", "dp"), None),
        ),
        out_specs=P(("groups", "dp"), None),
        check_vma=False,
    )
```

```python
import functools

import jax
import jax.numpy as jnp
from jax import lax
from jax.experimental import pallas as pl
from jax.experimental.pallas import tpu as pltpu
from jax.sharding import PartitionSpec as P

PANEL = 128
EX_DEV = 2
SUB = 16
LOOK = 10
Y_LAG = 3
USE_LAG = 5
EARLY = 2
F32 = jnp.float32


def remote(src, dst, send_sem, recv_sem, device):
    return pltpu.make_async_remote_copy(
        src_ref=src,
        dst_ref=dst,
        send_sem=send_sem,
        recv_sem=recv_sem,
        device_id=device,
        device_id_type=pl.DeviceIdType.MESH,
    )


def matmul_nt(a, b):
    return lax.dot_general(a, b, (((1,), (1,)), ((), ())), preferred_element_type=F32)


def kernel(
    dims,
    act_hbm,
    grad_hbm,
    ql_hbm,
    qr_hbm,
    live_ref,
    example_ref,
    out_ref,
    act,
    grad,
    ql,
    qr,
    first,
    first_in,
    unit,
    unit_in,
    sums,
    ends,
    load_sem,
    own_sem,
    sib_send,
    sib_recv,
    x_send,
    x_recv,
    xs_send,
    xs_recv,
    y_send,
    y_recv,
    ys_send,
    ys_recv,
    z_send,
    z_recv,
    end_send,
    end_recv,
):
    chips, owners, splits = dims
    pieces = splits + 1
    tokens = act.shape[0]
    share = tokens // owners
    width = act.shape[1] // splits
    g = lax.axis_index("groups")
    d = lax.axis_index("dp")
    o = lax.axis_index("owner")
    x = d // 2
    core = d % 2
    sibling = {"dp": 2 * x + 1 - core}
    across = {"groups": 1 - g}

    def columns(f):
        return pl.ds((f - 1) * width, width)

    def block(s, h, a, f):
        return ql.at[s, h, a] if f == 0 else qr.at[s, h, a, :, columns(f)]

    def whole_block(s, f):
        return ql.at[s] if f == 0 else qr.at[s, :, :, :, columns(f)]

    own_loads = [
        pltpu.make_async_copy(ql_hbm, ql.at[d], own_sem.at[0]),
        pltpu.make_async_copy(qr_hbm, qr.at[d], own_sem.at[1]),
    ]
    for copy in own_loads:
        copy.start()
    loads = [pltpu.make_async_copy(grad_hbm, grad, load_sem.at[0])]
    for f in range(1, pieces):
        loads.append(
            pltpu.make_async_copy(act_hbm.at[:, columns(f)], act.at[:, columns(f)], load_sem.at[f])
        )
    for copy in loads[:EARLY]:
        copy.start()

    barrier = pltpu.get_barrier_semaphore()
    peers = [sibling, across]
    peers += [{"dp": 2 * lax.rem(x + k, chips) + core} for k in range(1, chips)]
    peers += [{"owner": lax.rem(o + k, owners)} for k in range(1, owners)]
    for peer in peers:
        pl.semaphore_signal(barrier, inc=1, device_id=peer, device_id_type=pl.DeviceIdType.MESH)
    sums[...] = jnp.zeros_like(sums)
    for copy in own_loads:
        copy.wait()
    pl.semaphore_wait(barrier, len(peers))

    sends = []

    def send(src, dst, send_sem, recv_sem, device):
        copy = remote(src, dst, send_sem, recv_sem, device)
        copy.start()
        sends.append(copy)

    def arrived(ref, send_sem, recv_sem, device):
        remote(ref, ref, send_sem, recv_sem, device).wait_recv()

    order = [(k, a, f) for k in range(1, chips) for a in range(2) for f in range(pieces)]
    count = len(order)

    def send_across_x(i):
        if i < count:
            k, a, p = order[i]
            ref = block(d, g, a, p)
            send(ref, ref, x_send.at[i], x_recv.at[i], {"dp": 2 * lax.rem(x + k, chips) + core})

    for i in range(LOOK):
        send_across_x(i)
    for f in range(pieces):
        ref = whole_block(d, f)
        send(ref, ref, sib_send.at[f], sib_recv.at[f], sibling)
    for copy in loads[EARLY:]:
        copy.start()

    def chip_of(k):
        return lax.rem(x + chips - k, chips)

    def partial(u):
        return (first, first_in) if u == 0 else (unit.at[u - 1], unit_in.at[u - 1])

    def z_peer(k):
        return lax.rem(o + k, owners)

    def z_copy(u, k):
        total, incoming = partial(u)
        slot = u * owners + k
        rows = pl.ds(pl.multiple_of(z_peer(k) * share, share), share)
        return remote(
            total.at[rows],
            incoming.at[k - 1],
            z_send.at[slot],
            z_recv.at[slot],
            {"owner": z_peer(k)},
        )

    def scatter(u):
        for k in range(1, owners):
            z_copy(u, k).start()

    def finish(u):
        total, incoming = partial(u)
        for k in range(1, owners):
            z_copy(u, k).wait_recv()
        value = total[pl.ds(pl.multiple_of(o * share, share), share), :]
        for k in range(1, owners):
            value = value + incoming[k - 1]
        if value.shape[1] == 256:
            product = value[:, :128] * value[:, 128:]
        else:
            product = value * pltpu.roll(value, 64, 1)
        for start in range(0, share, min(share, PANEL)):
            rows = min(share, PANEL)
            token = o * share + start
            panel = token // PANEL
            position = lax.broadcasted_iota(jnp.int32, (rows, 128), 0) + token % PANEL
            kept = jnp.where(position < live_ref[0, panel], product[start : start + rows], 0.0)
            row = jnp.sum(kept, axis=0, keepdims=True)
            label = lax.broadcasted_iota(jnp.int32, (8, 128), 0)
            sums[u] = sums[u] + jnp.where(label == example_ref[0, panel], row, 0.0)

    units = 1 + 2 * (chips - 1)
    ready = {pieces - 1: 0}
    for u in range(1, units):
        ready[pieces * u - 1 + USE_LAG] = u

    for i in range(max(ready) + 1):
        if i < count:
            k, a, f = order[i]
            ref = block(2 * chip_of(k) + core, g, a, f)
            arrived(ref, x_send.at[i], x_recv.at[i], sibling)
            send_across_x(i + LOOK)
            send(ref, ref, y_send.at[i], y_recv.at[i], across)
            send(ref, ref, xs_send.at[i], xs_recv.at[i], sibling)
        if Y_LAG <= i < count + Y_LAG:
            k, a, f = order[i - Y_LAG]
            ref = block(2 * chip_of(k) + core, 1 - g, a, f)
            arrived(ref, y_send.at[i - Y_LAG], y_recv.at[i - Y_LAG], across)
            send(ref, ref, ys_send.at[i - Y_LAG], ys_recv.at[i - Y_LAG], sibling)
        if i < pieces:
            loads[i].wait()
            arrived(
                whole_block(2 * x + 1 - core, i), sib_send.at[i], sib_recv.at[i], sibling
            )
            if i == 0:
                rhs = ql[pl.ds(2 * x, 2)].reshape(128, ql.shape[-1])
                first[:, :128] = matmul_nt(grad[...], rhs)
            else:
                cols = columns(i)
                rhs = qr[pl.ds(2 * x, 2), :, :, :, cols].reshape(128, width)
                part = matmul_nt(act[:, cols], rhs)
                first[:, 128:] = part if i == 1 else first[:, 128:] + part
        if USE_LAG <= i < count + USE_LAG:
            k, a, f = order[i - USE_LAG]
            source = chip_of(k)
            other = 2 * source + 1 - core
            arrived(block(other, g, a, f), xs_send.at[i - USE_LAG], xs_recv.at[i - USE_LAG], sibling)
            arrived(block(other, 1 - g, a, f), ys_send.at[i - USE_LAG], ys_recv.at[i - USE_LAG], sibling)
            u = 2 * (k - 1) + a
            if f == 0:
                rhs = ql[pl.ds(2 * source, 2), :, a].reshape(64, ql.shape[-1])
                rhs = jnp.concatenate([rhs, jnp.zeros_like(rhs)], axis=0)
                unit[u] = matmul_nt(grad[...], rhs)
            else:
                cols = columns(f)
                rhs = qr[pl.ds(2 * source, 2), :, a, :, cols].reshape(64, width)
                rhs = jnp.concatenate([jnp.zeros_like(rhs), rhs], axis=0)
                if f < pieces - 1:
                    unit[u] = unit[u] + matmul_nt(act[:, cols], rhs)
                else:
                    for step in range(1, owners + 1):
                        rows = pl.ds(pl.multiple_of(z_peer(step) * share, share), share)
                        unit[u, rows] = unit[u, rows] + matmul_nt(act[rows, cols], rhs)
                        if step < owners:
                            z_copy(u + 1, step).start()
        if i == pieces - 1:
            scatter(0)

    for u in range(units):
        finish(u)

    lane = lax.broadcasted_iota(jnp.int32, (128, ends.shape[-1]), 0)
    query = lax.broadcasted_iota(jnp.int32, (128, ends.shape[-1]), 1)
    spread = (query == 16 * x + lane // 8).astype(F32)
    result = jnp.dot(
        sums[0], spread, precision=lax.Precision.HIGHEST, preferred_element_type=F32
    )
    for k in range(1, chips):
        for a in range(2):
            u = 1 + 2 * (k - 1) + a
            place = (lane // 32) * 8 + (lane % 32) // 16 * 4 + 2 * a + (lane % 16) // 8
            hit = (query == 16 * chip_of(k) + place) & (lane < 64)
            result = result + jnp.dot(
                sums[u],
                hit.astype(F32),
                precision=lax.Precision.HIGHEST,
                preferred_element_type=F32,
            )
    ends[o] = result
    end_copies = [
        remote(
            ends.at[o], ends.at[o], end_send.at[k], end_recv.at[k], {"owner": z_peer(k)}
        )
        for k in range(1, owners)
    ]
    for copy in end_copies:
        copy.start()
    for k in range(1, owners):
        arrived(ends.at[z_peer(owners - k)], end_send.at[k], end_recv.at[k], sibling)
    both = ends[0]
    for e in range(1, owners):
        both = both + ends[e]
    out_ref[...] = both[: out_ref.shape[0], : out_ref.shape[1]]

    for copy in sends:
        copy.wait_send()
    for u in range(units):
        for k in range(1, owners):
            z_copy(u, k).wait_send()
    for copy in end_copies:
        copy.wait_send()


def shards(sizes, hidden_act, out_grad, query_left, query_right, panel_live, panel_example):
    chips, owners = sizes
    tokens, units_here = hidden_act.shape
    feat_here = out_grad.shape[1]
    block, ranks, _ = query_left.shape
    splits = 4 if chips == 2 else 1
    pieces = splits + 1
    count = 2 * (chips - 1) * pieces
    units = 1 + 2 * (chips - 1)
    queries = block * 2 * chips
    wide = -(-queries // 128) * 128
    share = tokens // owners
    ql = query_left.reshape(2, 2, SUB, feat_here)
    qr = query_right.reshape(2, 2, SUB, units_here)
    dma = pltpu.SemaphoreType.DMA
    anywhere = pl.BlockSpec(memory_space=pl.ANY)
    smem = pl.BlockSpec(memory_space=pltpu.SMEM)
    return pl.pallas_call(
        functools.partial(kernel, (chips, owners, splits)),
        out_shape=jax.ShapeDtypeStruct((EX_DEV, queries), F32),
        in_specs=[anywhere] * 4 + [smem] * 2,
        out_specs=pl.BlockSpec(memory_space=pltpu.VMEM),
        scratch_shapes=[
            pltpu.VMEM((tokens, units_here), jnp.bfloat16),
            pltpu.VMEM((tokens, feat_here), jnp.bfloat16),
            pltpu.VMEM((2 * chips, 2, 2, SUB, feat_here), jnp.bfloat16),
            pltpu.VMEM((2 * chips, 2, 2, SUB, units_here), jnp.bfloat16),
            pltpu.VMEM((tokens, 256), F32),
            pltpu.VMEM((owners - 1, share, 256), F32),
            pltpu.VMEM((units - 1, tokens, 128), F32),
            pltpu.VMEM((units - 1, owners - 1, share, 128), F32),
            pltpu.VMEM((units, 8, 128), F32),
            pltpu.VMEM((owners, 8, wide), F32),
            dma((pieces,)),
            dma((2,)),
            dma((pieces,)),
            dma((pieces,)),
        ]
        + [dma((count,))] * 8
        + [
            dma((units * owners,)),
            dma((units * owners,)),
            dma((owners,)),
            dma((owners,)),
        ],
        compiler_params=pltpu.CompilerParams(
            collective_id=0, has_side_effects=True, vmem_limit_bytes=56 * 1024 * 1024
        ),
    )(hidden_act, out_grad, ql, qr, panel_live, panel_example)


def solution(mesh):
    sizes = (mesh.shape["dp"] // 2, mesh.shape["owner"])
    return jax.shard_map(
        functools.partial(shards, sizes),
        mesh=mesh,
        in_specs=(
            P(("groups", "dp"), "owner"),
            P(("groups", "dp"), "owner"),
            P("dp", None, "owner"),
            P("dp", None, "owner"),
            P(("groups", "dp"), None),
            P(("groups", "dp"), None),
        ),
        out_specs=P(("groups", "dp"), None),
        check_vma=False,
    )
```
